32 devices in a mesh: ctx: 8 (over z, core), tp: 4 (over y, x).
Axes of the slice: x: 2, y: 2, z: 4, core: 2. Of those that a mesh axis runs over, the one named last changes fastest.
Arguments:
- query_latent: bfloat16 [4096, 64, 512], P('ctx', 'tp'), may hold values from -24 to 24
- query_rope: bfloat16 [4096, 4096], P('ctx', 'tp'), may hold values from -24 to 24
- key_latent: bfloat16 [4096, 512], P('ctx'), may hold values from -6 to 6
- key_rope: bfloat16 [2048, 128], P('ctx'), may hold values from -6 to 6
- block_ids: int32 [16], replicated, may hold values from 0 to 15, as said below
- value_up: bfloat16 [64, 512, 128], P('tp'), may hold values from -0.5 to 0.5
- out_weight: bfloat16 [8192, 7168], P('tp'), may hold values from -0.0625 to 0.0625
- residual: bfloat16 [4096, 7168], P(('ctx', 'tp')), may hold values from -18 to 18
- norm_gain: float32 [7168], replicated, may hold values from 0.1 to 1.9
- gate_weight: bfloat16 [7168, 2048], P('ctx', 'tp'), may hold values from -0.0625 to 0.0625
- up_weight: bfloat16 [7168, 2048], P('ctx', 'tp'), may hold values from -0.0625 to 0.0625
- down_weight: bfloat16 [7168, 2048], P('ctx', 'tp'), may hold values from -0.125 to 0.125
Outputs:
- layer_out: bfloat16 [4096, 7168], P(('ctx', 'tp'))
The draws below stay inside these ranges and needn't reach their ends.
Inputs may be any that keep to these rules, and one draw needn't show every extreme that they name: `block_ids`: index c of ctx stores blocks 2c and 2c + 1; their two entries sum to 15, and every value appears once.
All inputs are finite; a program needn't handle non-finite values.
Results may differ from the reference program's by a relative error of at most 0.018.
Values may be sent and summed in bfloat16 or wider, within the bound.
A program may use at most 192 MiB of HBM per device.

```python
import math
import jax
import jax.numpy as jnp
from jax import lax

D = 7168
FF = 2048
H = 64
LATENT = 512
ROPE = 64
VDIM = 128
TOKENS = 4096
BLOCKS = 16
N_CTX = 8
N_TP = 4


def latent_keys(key):
    draw_key = jax.random.fold_in(key, 101)
    width = LATENT + ROPE
    return jnp.clip(jax.random.normal(draw_key, (TOKENS, width), jnp.float32), -6.0, 6.0)


def query_fields(key):
    width = LATENT + ROPE
    draw_key = jax.random.fold_in(key, 202)
    return jnp.clip(jax.random.normal(draw_key, (TOKENS, H, width), jnp.float32), -6.0, 6.0)


def draw_query_latent(key, part):
    return query_fields(key)[:, :, :LATENT].astype(jnp.bfloat16)


def draw_query_rope(key, part):
    return query_fields(key)[:, :, LATENT:].reshape(TOKENS, H * ROPE).astype(jnp.bfloat16)


def draw_key_latent(key, part):
    return latent_keys(key)[:, :LATENT].astype(jnp.bfloat16)


def draw_key_rope(key, part):
    return latent_keys(key)[:, LATENT:].reshape(TOKENS // 2, 2 * ROPE).astype(jnp.bfloat16)


def draw_block_ids(key, part):
    pair_count = BLOCKS // 2
    shuffled = jax.random.permutation(jax.random.fold_in(key, 7), pair_count)
    flipped = jax.random.randint(jax.random.fold_in(key, 8), (pair_count,), 0, 2)
    low_block = shuffled
    high_block = BLOCKS - 1 - shuffled
    first_block = jnp.where(flipped == 1, high_block, low_block)
    second_block = jnp.where(flipped == 1, low_block, high_block)
    return jnp.stack([first_block, second_block], axis=1).reshape(BLOCKS).astype(jnp.int32)


def draw_residual(key, part):
    col_scale = jnp.exp(jax.random.uniform(jax.random.fold_in(key, 31), (D,), jnp.float32, math.log(0.3), math.log(3.0)))
    base_draw = jnp.clip(jax.random.normal(jax.random.fold_in(key, 33), (TOKENS, D), jnp.float32), -6.0, 6.0)
    values = base_draw * col_scale[None, :]
    return values.astype(jnp.bfloat16)


def level_of(key, extent, split, smallest, top_value):
    def one(position, blocks):
        steps = jax.random.uniform(jax.random.fold_in(jax.random.fold_in(key, 6), position), (blocks,), jnp.float32, smallest / len(split), top_value / len(split))
        return jnp.repeat(jnp.exp(steps), extent[position] // blocks).reshape((-1,) + (1,) * (len(extent) - position - 1))

    level = one(*split[0])
    for cut in split[1:]:
        level = level * one(*cut)
    return level


def centred(key, shape, spread, reach, pieces=(), held_as=jnp.bfloat16):
    entries = spread * jax.random.normal(key, shape, jnp.float32)
    if pieces:
        entries = entries * level_of(key, shape, pieces, -0.22, 0.18)
    return jnp.clip(entries, -reach, reach).astype(held_as)


def setup_inputs(seed: int = 0) -> dict:
    key_list = jax.random.split(jax.random.key(seed), 13)
    query_latent = draw_query_latent(jax.random.fold_in(key_list[12], 71), 0)
    query_rope = draw_query_rope(jax.random.fold_in(key_list[12], 71), 0)
    key_latent = draw_key_latent(jax.random.fold_in(key_list[12], 71), 0)
    key_rope = draw_key_rope(jax.random.fold_in(key_list[12], 71), 0)
    block_ids = draw_block_ids(jax.random.fold_in(key_list[12], 71), 0)
    value_up = centred(key_list[5], (H, LATENT, VDIM), VDIM ** -0.5, 0.5, ((0, 4),))
    out_weight = centred(key_list[6], (H * VDIM, D), (H * VDIM) ** -0.5, 0.0625, ((0, 4),))
    residual = draw_residual(jax.random.fold_in(key_list[12], 71), 0)
    norm_gain = jnp.clip(1.0 + 0.18 * jax.random.normal(key_list[8], (D,), jnp.float32), 0.1, 1.9)
    gate_weight = centred(key_list[9], (D, FF), D ** -0.5, 0.0625, ((0, 8), (1, 4)))
    up_weight = centred(key_list[10], (D, FF), D ** -0.5, 0.0625, ((0, 8), (1, 4)))
    down_weight = centred(key_list[11], (D, FF), FF ** -0.5, 0.125, ((0, 8), (1, 4)))
    return dict(query_latent=query_latent, query_rope=query_rope, key_latent=key_latent, key_rope=key_rope, block_ids=block_ids, value_up=value_up, out_weight=out_weight, residual=residual, norm_gain=norm_gain, gate_weight=gate_weight, up_weight=up_weight, down_weight=down_weight)


def rms_norm(activation, gain_vector):
    mean_square = lax.optimization_barrier(jnp.mean(activation * activation, axis=-1, keepdims=True))
    return (activation * lax.rsqrt(mean_square + 1e-06) * gain_vector).astype(jnp.bfloat16)

def reference(query_latent, query_rope, key_latent, key_rope, block_ids, value_up, out_weight, residual, norm_gain, gate_weight, up_weight, down_weight):
    total_rows = key_latent.shape[0]
    seq_rows = total_rows // N_CTX
    half_len = seq_rows // 2
    head_count = query_latent.shape[1]
    score_scale = (VDIM + ROPE) ** (-0.5)
    rope_keys = key_rope.reshape(total_rows, ROPE)
    rope_queries = query_rope.reshape(total_rows, head_count, ROPE)
    row_index = jnp.arange(total_rows, dtype=jnp.int32)
    positions = (block_ids[row_index // half_len] * half_len + row_index % half_len).astype(jnp.int32)

    def one_device(device):
        row_start = (device * seq_rows).astype(jnp.int32)
        prev_start = ((device + N_CTX - 1) % N_CTX * seq_rows).astype(jnp.int32)
        lat_block = lax.dynamic_slice_in_dim(query_latent, row_start, seq_rows, 0).astype(jnp.float32)
        rope_block = lax.dynamic_slice_in_dim(rope_queries, row_start, seq_rows, 0).astype(jnp.float32)
        keys_lat = jnp.concatenate([lax.dynamic_slice_in_dim(key_latent, row_start, seq_rows, 0), lax.dynamic_slice_in_dim(key_latent, prev_start, seq_rows, 0)], axis=0).astype(jnp.float32)
        keys_rot = jnp.concatenate([lax.dynamic_slice_in_dim(rope_keys, row_start, seq_rows, 0), lax.dynamic_slice_in_dim(rope_keys, prev_start, seq_rows, 0)], axis=0).astype(jnp.float32)
        query_pos = lax.dynamic_slice_in_dim(positions, row_start, seq_rows, 0)
        key_pos = jnp.concatenate([query_pos, lax.dynamic_slice_in_dim(positions, prev_start, seq_rows, 0)], axis=0)
        scores = jnp.einsum('shl,kl->hsk', lat_block, keys_lat) + jnp.einsum('shr,kr->hsk', rope_block, keys_rot)
        scores = scores * score_scale
        visible = key_pos[None, :] <= query_pos[:, None]
        scores = jnp.where(visible[None], scores, -jnp.inf)
        highest = lax.optimization_barrier(jnp.max(scores, axis=-1, keepdims=True))
        exponent = jnp.exp(scores - highest)
        weights = (exponent / lax.optimization_barrier(jnp.sum(exponent, axis=-1, keepdims=True))).astype(jnp.bfloat16)
        blended = jnp.einsum('hsk,kl->shl', weights.astype(jnp.float32), keys_lat).astype(jnp.bfloat16)
        values = jnp.einsum('shl,hlv->shv', blended.astype(jnp.float32), value_up.astype(jnp.float32)).astype(jnp.bfloat16)
        return values.reshape(seq_rows, head_count * VDIM)
    head_out = lax.map(one_device, jnp.arange(N_CTX, dtype=jnp.int32)).reshape(total_rows, head_count * VDIM)
    group_cols = head_count * VDIM // N_TP

    def add_attn(group_index, running):
        begin_col = (group_index * group_cols).astype(jnp.int32)
        col_block = lax.dynamic_slice_in_dim(head_out, begin_col, group_cols, 1)
        row_block = lax.dynamic_slice_in_dim(out_weight, begin_col, group_cols, 0)
        partial_value = jnp.dot(col_block, row_block, preferred_element_type=jnp.float32).astype(jnp.bfloat16)
        return running + lax.optimization_barrier(partial_value).astype(jnp.float32)
    attn_total = lax.fori_loop(0, N_TP, add_attn, jnp.zeros((total_rows, D), jnp.float32))
    hidden_state = residual.astype(jnp.float32) + attn_total
    normed = rms_norm(hidden_state, norm_gain)
    gate_proj = jnp.dot(normed, gate_weight, preferred_element_type=jnp.float32)
    up_proj = jnp.dot(normed, up_weight, preferred_element_type=jnp.float32)
    hidden_units = (jax.nn.silu(gate_proj) * up_proj).astype(jnp.bfloat16)
    unit_cols = FF // N_TP

    def add_shared(group_index, running):
        begin_col = (group_index * unit_cols).astype(jnp.int32)
        col_block = lax.dynamic_slice_in_dim(hidden_units, begin_col, unit_cols, 1)
        row_block = lax.dynamic_slice_in_dim(down_weight, begin_col, unit_cols, 1)
        partial_value = lax.dot_general(col_block, row_block, (((1,), (1,)), ((), ())), preferred_element_type=jnp.float32).astype(jnp.bfloat16)
        return running + lax.optimization_barrier(partial_value).astype(jnp.float32)
    shared_total = lax.fori_loop(0, N_TP, add_shared, jnp.zeros((total_rows, D), jnp.float32))
    return (hidden_state + shared_total).astype(jnp.bfloat16)
```

```python
import jax
import jax.numpy as jnp
from jax import lax
from jax.sharding import PartitionSpec as P


def from_behind(x, axis, by):
    length = lax.axis_size(axis)
    return lax.ppermute(x, axis, [(i, (i + by) % length) for i in range(length)])


def rms_norm(activation, gain_vector):
    mean_square = jnp.mean(activation * activation, axis=-1, keepdims=True)
    return (activation * lax.rsqrt(mean_square + 1e-06) * gain_vector).astype(jnp.bfloat16)


def swap(x, bit):
    length = lax.axis_size("tp")
    return lax.ppermute(x, "tp", [(i, i ^ bit) for i in range(length)])


def owner_rows(x, owner, part, share_rows):
    half = share_rows // 2
    return lax.dynamic_slice_in_dim(x, owner * share_rows + part * half, half, 0)


def scatter_sum(rows, product, share_rows, pin, indexed=True):
    me = lax.axis_index("tp") if indexed else 0
    half = share_rows // 2

    def pick(owner, part):
        return owner_rows(rows, owner, part, share_rows)

    give = jnp.concatenate([pick(me ^ 3, 0), pick(me ^ 1, 0), pick(me ^ 3, 1), pick(me ^ 2, 1)], axis=0)
    keep = jnp.concatenate([pick(me ^ 2, 0), pick(me, 0), pick(me ^ 1, 1), pick(me, 1)], axis=0)
    give, keep = lax.optimization_barrier((give, keep))
    sent = product(give)
    got_a = swap(sent[: 2 * half], 1)
    got_b = swap(sent[2 * half :], 2)
    keep, _ = lax.optimization_barrier((keep, sent))
    kept = product(pin(keep))
    far_a = (kept[:half].astype(jnp.float32) + got_a[:half].astype(jnp.float32)).astype(jnp.bfloat16)
    far_b = (
        kept[2 * half : 3 * half].astype(jnp.float32) + got_b[:half].astype(jnp.float32)
    ).astype(jnp.bfloat16)
    last_a = swap(far_a, 2)
    last_b = swap(far_b, 1)
    near_a = kept[half : 2 * half].astype(jnp.float32) + got_a[half:].astype(jnp.float32)
    near_b = kept[3 * half :].astype(jnp.float32) + got_b[half:].astype(jnp.float32)
    return near_a + last_a.astype(jnp.float32), near_b + last_b.astype(jnp.float32)


def gather_rows(own):
    half = own.shape[0] // 2
    own_a, own_b = own[:half], own[half:]
    side_a = swap(own_a, 1)
    side_b = swap(own_b, 2)
    far_own_a, far_side_a = swap(own_a, 2), swap(side_a, 2)
    far_own_b, far_side_b = swap(own_b, 1), swap(side_b, 1)
    blocks = [
        jnp.concatenate([own_a, own_b], axis=0),
        jnp.concatenate([side_a, far_own_b], axis=0),
        jnp.concatenate([far_own_a, side_b], axis=0),
        jnp.concatenate([far_side_a, far_side_b], axis=0),
    ]
    return jnp.concatenate(blocks, axis=0)


def local(
    query_latent,
    query_rope,
    key_latent,
    key_rope,
    block_ids,
    value_up,
    out_weight,
    residual,
    norm_gain,
    gate_weight,
    up_weight,
    down_weight,
):
    seq_rows = key_latent.shape[0]
    half_len = seq_rows // 2
    head_count = query_latent.shape[1]
    rope_dim = key_rope.shape[1] // 2
    head_dim = value_up.shape[2]
    ctx_count = lax.axis_size("ctx")
    score_scale = (head_dim + rope_dim) ** (-0.5)
    recv_latent, recv_rope = from_behind((key_latent, key_rope), "ctx", 1)
    keys_lat = jnp.concatenate([key_latent, recv_latent], axis=0)
    keys_rot = jnp.concatenate(
        [key_rope.reshape(seq_rows, rope_dim), recv_rope.reshape(seq_rows, rope_dim)], axis=0
    )
    current = lax.axis_index("ctx")
    previous = (current + ctx_count - 1) % ctx_count
    own_ids = lax.dynamic_slice_in_dim(block_ids, current * 2, 2, 0)
    prev_ids = lax.dynamic_slice_in_dim(block_ids, previous * 2, 2, 0)
    row_index = jnp.arange(seq_rows, dtype=jnp.int32)
    first_half = row_index < half_len
    offset = row_index % half_len
    query_pos = jnp.where(first_half, own_ids[0], own_ids[1]) * half_len + offset
    key_pos = jnp.concatenate(
        [query_pos, jnp.where(first_half, prev_ids[0], prev_ids[1]) * half_len + offset], axis=0
    )
    rope_queries = query_rope.reshape(seq_rows, head_count, rope_dim)
    block_rows = min(seq_rows, 512)

    def attend(block_index):
        scores = jnp.einsum(
            "shl,kl->hsk", query_latent, keys_lat, preferred_element_type=jnp.float32
        )
        scores = scores + jnp.einsum(
            "shr,kr->hsk", rope_queries, keys_rot, preferred_element_type=jnp.float32
        )
        scores = scores * score_scale
        visible = key_pos[None, :] <= query_pos[:, None]
        scores = jnp.where(visible[None], scores, -jnp.inf)
        highest = jnp.max(scores, axis=-1, keepdims=True)
        exponent = jnp.exp(scores - highest)
        weights = (exponent / jnp.sum(exponent, axis=-1, keepdims=True)).astype(jnp.bfloat16)
        blended = jnp.einsum(
            "hsk,kl->shl", weights, keys_lat, preferred_element_type=jnp.float32
        ).astype(jnp.bfloat16)
        values = jnp.einsum(
            "shl,hlv->shv", blended, value_up, preferred_element_type=jnp.float32
        ).astype(jnp.bfloat16)
        return values.reshape(block_rows, head_count * head_dim)

    head_out = lax.map(attend, jnp.arange(seq_rows // block_rows, dtype=jnp.int32)).reshape(
        seq_rows, head_count * head_dim
    )
    share_rows = seq_rows // lax.axis_size("tp")
    gate_full = lax.all_gather(gate_weight, "ctx", axis=0, tiled=True)
    up_in, gate_full = lax.optimization_barrier((up_weight, gate_full))
    up_full = lax.all_gather(up_in, "ctx", axis=0, tiled=True)
    down_in, up_full = lax.optimization_barrier((down_weight, up_full))
    down_full = lax.all_gather(down_in, "ctx", axis=0, tiled=True)

    def project(rows):
        return jnp.dot(rows, out_weight, preferred_element_type=jnp.float32).astype(jnp.bfloat16)

    def pin(rows):
        return lax.optimization_barrier((rows, gate_full))[0]

    attn_a, attn_b = scatter_sum(head_out, project, share_rows, pin)
    attn_total = jnp.concatenate([attn_a, attn_b], axis=0)
    own_state = residual.astype(jnp.float32) + attn_total
    normed_own = rms_norm(own_state, norm_gain)
    normed_own, up_full = lax.optimization_barrier((normed_own, up_full))
    normed_all = gather_rows(normed_own)
    gate_proj = jnp.dot(normed_all, gate_full, preferred_element_type=jnp.float32)
    up_proj = jnp.dot(normed_all, up_full, preferred_element_type=jnp.float32)
    hidden_units = (jax.nn.silu(gate_proj) * up_proj).astype(jnp.bfloat16)

    def expand(rows):
        return lax.dot_general(
            rows, down_full, (((1,), (1,)), ((), ())), preferred_element_type=jnp.float32
        ).astype(jnp.bfloat16)

    shared_a, shared_b = scatter_sum(hidden_units, expand, share_rows, lambda rows: rows, False)
    shared_part = jnp.concatenate([shared_a, shared_b], axis=0)
    return (own_state + shared_part).astype(jnp.bfloat16)


def solution(mesh):
    placed = (
        P("ctx", "tp", None),
        P("ctx", "tp"),
        P("ctx", None),
        P("ctx", None),
        P(),
        P("tp", None, None),
        P("tp", None),
        P(("ctx", "tp"), None),
        P(),
        P("ctx", "tp"),
        P("ctx", "tp"),
        P("ctx", "tp"),
    )
    return jax.shard_map(
        local, mesh=mesh, in_specs=placed, out_specs=P(("ctx", "tp"), None), check_vma=False
    )
```

```python
import functools
import math

import jax
import jax.numpy as jnp
from jax import lax
from jax.experimental import pallas as pl
from jax.experimental.pallas import tpu as pltpu
from jax.sharding import PartitionSpec as P


def from_behind(x, axis, by):
    length = lax.axis_size(axis)
    return lax.ppermute(x, axis, [(i, (i + by) % length) for i in range(length)])


def rms_norm(activation, gain_vector):
    mean_square = jnp.mean(activation * activation, axis=-1, keepdims=True)
    return (activation * lax.rsqrt(mean_square + 1e-06) * gain_vector).astype(jnp.bfloat16)


def swap(x, bit):
    length = lax.axis_size("tp")
    return lax.ppermute(x, "tp", [(i, i ^ bit) for i in range(length)])


def scatter_sum(product, half):
    sent = product(((3, 0), (1, 0), (3, 1), (2, 1)), None)
    sent_a, sent_b = lax.optimization_barrier((sent[: 2 * half], sent[2 * half :]))
    got_a = swap(sent_a, 1)
    got_b = swap(sent_b, 2)
    kept = product(((2, 0), (0, 0), (1, 1), (0, 1)), sent_a)
    got_a, got_b, kept = lax.optimization_barrier((got_a, got_b, kept))
    far_a = (kept[:half].astype(jnp.float32) + got_a[:half].astype(jnp.float32)).astype(jnp.bfloat16)
    far_b = (
        kept[2 * half : 3 * half].astype(jnp.float32) + got_b[:half].astype(jnp.float32)
    ).astype(jnp.bfloat16)
    far_a, far_b = lax.optimization_barrier((far_a, far_b))
    last_a, last_b = lax.optimization_barrier((swap(far_a, 2), swap(far_b, 1)))
    near_a = kept[half : 2 * half].astype(jnp.float32) + got_a[half:].astype(jnp.float32)
    near_b = kept[3 * half :].astype(jnp.float32) + got_b[half:].astype(jnp.float32)
    return near_a + last_a.astype(jnp.float32), near_b + last_b.astype(jnp.float32)


def gather_rows(own):
    half = own.shape[0] // 2
    own_a, own_b = own[:half], own[half:]
    side_a = swap(own_a, 1)
    side_b = swap(own_b, 2)
    far_own_a, far_side_a = swap(own_a, 2), swap(side_a, 2)
    far_own_b, far_side_b = swap(own_b, 1), swap(side_b, 1)
    blocks = [
        jnp.concatenate([own_a, own_b], axis=0),
        jnp.concatenate([side_a, far_own_b], axis=0),
        jnp.concatenate([far_own_a, side_b], axis=0),
        jnp.concatenate([far_side_a, far_side_b], axis=0),
    ]
    return jnp.concatenate(blocks, axis=0)


def attend_kernel(
    heads, half_len, scale, tile, order, sizes, query, rope, keys_t, rope_t, keys, out
):
    step = pl.program_id(0)
    steps = pl.num_programs(0) // order.shape[0]
    block = order[step // steps]
    rows = query.shape[0]
    first_token = ((block * steps + step % steps) * (rows // heads)) % half_len
    unit = keys.shape[0] // 4

    def work(count):
        width = count * unit
        begin = 0 if count <= 2 else 2 * unit
        for start in range(0, rows, tile):
            part = pl.ds(start, tile)
            scores = jnp.dot(query[part, :], keys_t[:, :width], preferred_element_type=jnp.float32)
            scores = scores + jnp.dot(
                rope[part, :], rope_t[:, :width], preferred_element_type=jnp.float32
            )
            token = first_token + (
                start + lax.broadcasted_iota(jnp.int32, (tile, unit), 0)
            ) // heads
            visible = lax.broadcasted_iota(jnp.int32, (tile, unit), 1) <= token
            pieces = [scores[:, begin : begin + unit]]
            pieces[0] = jnp.where(visible, pieces[0], -1e30)
            if begin:
                pieces.insert(0, scores[:, :begin])
            if begin + unit < width:
                pieces.append(scores[:, begin + unit :])
            scores = jnp.concatenate(pieces, axis=1)
            highest = jnp.max(scores, axis=1, keepdims=True)
            exponent = jnp.exp2((scores - highest) * (scale * math.log2(math.e)))
            total = jnp.sum(exponent, axis=1, keepdims=True)
            mixed = jnp.dot(
                exponent.astype(jnp.bfloat16), keys[:width, :], preferred_element_type=jnp.float32
            )
            out[part, :] = (mixed / total).astype(jnp.bfloat16)

    for count in (1, 2, 3, 4):
        pl.when(sizes[step // steps] == count)(functools.partial(work, count))


def attend_rows(order, sizes, heads, half_len, scale, query, rope, keys_t, rope_t, keys, block_rows):
    rows, tile = 512, 256
    latent = query.shape[1]
    steps = block_rows // rows
    count = order.shape[0]

    def index(i, order, sizes):
        return order[i // steps] * steps + i % steps, 0

    def whole(i, order, sizes):
        return 0, 0

    return pl.pallas_call(
        functools.partial(attend_kernel, heads, half_len, scale, tile),
        grid_spec=pltpu.PrefetchScalarGridSpec(
            num_scalar_prefetch=2,
            grid=(count * steps,),
            in_specs=[
                pl.BlockSpec((rows, latent), index),
                pl.BlockSpec((rows, rope.shape[1]), index),
                pl.BlockSpec(keys_t.shape, whole),
                pl.BlockSpec(rope_t.shape, whole),
                pl.BlockSpec(keys.shape, whole),
            ],
            out_specs=pl.BlockSpec((rows, latent), lambda i, order, sizes: (i, 0)),
        ),
        out_shape=jax.ShapeDtypeStruct((count * block_rows, latent), jnp.bfloat16),
        compiler_params=pltpu.CompilerParams(vmem_limit_bytes=48 * 2**20),
        cost_estimate=pl.CostEstimate(
            flops=1000,
            bytes_accessed=1000,
            transcendentals=0,
        ),
    )(order, sizes, query, rope, keys_t, rope_t, keys)


def project_kernel(rows, weight, out):
    out[...] = jnp.dot(
        rows[...], weight[...], preferred_element_type=jnp.float32
    ).astype(jnp.bfloat16)


def project(rows, weight):
    count, depth = rows.shape
    width = weight.shape[1]
    tile = math.gcd(width, 512)
    return pl.pallas_call(
        project_kernel,
        grid=(width // tile,),
        in_specs=[
            pl.BlockSpec((count, depth), lambda i: (0, 0)),
            pl.BlockSpec((depth, tile), lambda i: (0, i)),
        ],
        out_specs=pl.BlockSpec((count, tile), lambda i: (0, i)),
        out_shape=jax.ShapeDtypeStruct((count, width), jnp.bfloat16),
        compiler_params=pltpu.CompilerParams(vmem_limit_bytes=32 * 2**20),
        cost_estimate=pl.CostEstimate(flops=1000, bytes_accessed=1000, transcendentals=0),
    )(rows, weight)


def local(
    query_latent,
    query_rope,
    key_latent,
    key_rope,
    block_ids,
    value_up,
    out_weight,
    residual,
    norm_gain,
    gate_weight,
    up_weight,
    down_weight,
):
    seq_rows = key_latent.shape[0]
    half_len = seq_rows // 2
    head_count = query_latent.shape[1]
    rope_dim = key_rope.shape[1] // 2
    head_dim = value_up.shape[2]
    ctx_count = lax.axis_size("ctx")
    score_scale = (head_dim + rope_dim) ** (-0.5)
    recv_latent, recv_rope = from_behind((key_latent, key_rope), "ctx", 1)
    current = lax.axis_index("ctx")
    previous = (current + ctx_count - 1) % ctx_count
    own_ids = lax.dynamic_slice_in_dim(block_ids, current * 2, 2, 0)
    prev_ids = lax.dynamic_slice_in_dim(block_ids, previous * 2, 2, 0)
    own_low = (own_ids[0] > own_ids[1]).astype(jnp.int32)
    prev_low = (prev_ids[0] > prev_ids[1]).astype(jnp.int32)

    def ordered(own, prev):
        def pick(x, which):
            return lax.dynamic_slice_in_dim(x, which * half_len, half_len, 0)

        return jnp.concatenate(
            [pick(own, own_low), pick(prev, prev_low), pick(own, 1 - own_low), pick(prev, 1 - prev_low)],
            axis=0,
        )

    keys_lat = ordered(key_latent, recv_latent)
    keys_rot = ordered(
        key_rope.reshape(seq_rows, rope_dim), recv_rope.reshape(seq_rows, rope_dim)
    )
    keys_t, rope_t = keys_lat.T, keys_rot.T
    low_size = 1 + (jnp.min(prev_ids) < jnp.min(own_ids)).astype(jnp.int32)
    high_size = 3 + (jnp.max(prev_ids) < jnp.max(own_ids)).astype(jnp.int32)
    latent_rows = query_latent.reshape(seq_rows * head_count, query_latent.shape[2])
    rope_rows = query_rope.reshape(seq_rows * head_count, rope_dim)
    me = lax.axis_index("tp")
    share_rows = seq_rows // lax.axis_size("tp")
    unit_count = gate_weight.shape[1]
    weights = lax.optimization_barrier(
        jnp.concatenate([gate_weight, up_weight, down_weight], axis=1)
    )
    weights_full = lax.all_gather(weights, "ctx", axis=0, tiled=True)
    half = share_rows // 2

    def attention_term(pairs, after):
        order = jnp.stack([(me ^ owner) * 2 + part for owner, part in pairs])
        in_second = (order * half >= half_len).astype(jnp.int32)
        sizes = jnp.where(in_second == own_low, low_size, high_size)
        query = latent_rows
        if after is not None:
            query, _ = lax.optimization_barrier((query, after))
        blended = attend_rows(
            order, sizes, head_count, half_len, score_scale,
            query, rope_rows, keys_t, rope_t, keys_lat, half * head_count,
        )
        values = jnp.einsum(
            "shl,hlv->shv",
            blended.reshape(len(pairs) * half, head_count, -1),
            value_up,
            preferred_element_type=jnp.float32,
        ).astype(jnp.bfloat16)
        values = values.reshape(len(pairs) * half, head_count * head_dim)
        if after is None:
            return jnp.dot(values, out_weight, preferred_element_type=jnp.float32).astype(jnp.bfloat16)
        return project(values, out_weight)

    attn_a, attn_b = scatter_sum(attention_term, half)
    attn_total = jnp.concatenate([attn_a, attn_b], axis=0)
    own_state = residual.astype(jnp.float32) + attn_total
    normed_own = rms_norm(own_state, norm_gain)
    normed_all = gather_rows(normed_own)
    both = jnp.dot(
        normed_all, weights_full[:, : 2 * unit_count], preferred_element_type=jnp.float32
    )
    gate_proj, up_proj = both[:, :unit_count], both[:, unit_count:]
    hidden_units = (jax.nn.silu(gate_proj) * up_proj).astype(jnp.bfloat16)
    down_full = weights_full[:, 2 * unit_count :]

    def expert_term(pairs, after):
        rows = jnp.concatenate(
            [
                hidden_units[owner * share_rows + part * half : owner * share_rows + (part + 1) * half]
                for owner, part in pairs
            ],
            axis=0,
        )
        if after is not None:
            rows, _ = lax.optimization_barrier((rows, after))
        return lax.dot_general(
            rows, down_full, (((1,), (1,)), ((), ())), preferred_element_type=jnp.float32
        ).astype(jnp.bfloat16)

    shared_a, shared_b = scatter_sum(expert_term, half)
    shared_part = jnp.concatenate([shared_a, shared_b], axis=0)
    return (own_state + shared_part).astype(jnp.bfloat16)


def solution(mesh):
    placed = (
        P("ctx", "tp", None),
        P("ctx", "tp"),
        P("ctx", None),
        P("ctx", None),
        P(),
        P("tp", None, None),
        P("tp", None),
        P(("ctx", "tp"), None),
        P(),
        P("ctx", "tp"),
        P("ctx", "tp"),
        P("ctx", "tp"),
    )
    return jax.shard_map(
        local, mesh=mesh, in_specs=placed, out_specs=P(("ctx", "tp"), None), check_vma=False
    )
```
